32 devices in a mesh: tm: 8 (over z, x), rows: 4 (over y, core).
Axes of the slice: x: 2, y: 2, z: 4, core: 2. Of those that a mesh axis runs over, the one named last changes fastest.
Arguments:
- diag_blocks: float32 [16, 512, 512], P('tm', 'rows'), may hold values from -1 to 3.5, as said below
- coupling: float32 [16, 512, 512], P('tm', 'rows'), may hold values from -1.75 to 0.5
- rhs: float32 [16, 512], P('tm', 'rows'), may hold values from -0.25 to 0.25
Outputs:
- solution: float32 [16, 512], P('tm', 'rows')
- logdet_mean: float32 [], replicated
The draws below stay inside these ranges and needn't reach their ends.
Inputs may be any that keep to these rules, and one draw needn't show every extreme that they name: Every diag_blocks[t] is symmetric, and A is positive definite.
All inputs are finite; a program needn't handle non-finite values.
Results may differ from the reference program's by a relative error of at most 0.0003.
Values sent between devices are 32-bit elements; how exact they have to be, the bound alone decides.
A program may use at most 128 MiB of HBM per device.

```python
import math
import jax
import jax.numpy as jnp
from jax import lax

STATE = 512
HORIZON_LENGTH = 16


def smoother_parts(key):
    stochastic_seeds = [jax.random.fold_in(key, 101 + number) for number in range(8)]
    points = jax.random.uniform(stochastic_seeds[0], (HORIZON_LENGTH, STATE, 4), jnp.float32)
    signs = jnp.where(jax.random.bernoulli(stochastic_seeds[1], 0.5, (HORIZON_LENGTH, STATE)), 1.0, -1.0).astype(jnp.float32)
    kernel = jnp.ones((HORIZON_LENGTH, STATE, STATE), jnp.float32)
    for dim_index in range(4):
        gap = points[:, :, None, dim_index] - points[:, None, :, dim_index]
        kernel = kernel * jnp.exp(-jnp.abs(gap) / 0.5) * jnp.cos(6.0 * gap)
    kernel = kernel * signs[:, :, None] * signs[:, None, :]
    kernel = 0.5 * (kernel + jnp.swapaxes(kernel, 1, 2))
    prec_diag = jax.random.uniform(stochastic_seeds[2], (HORIZON_LENGTH, STATE), jnp.float32, 0.8, 1.2)
    base_rate = jnp.exp(jax.random.uniform(stochastic_seeds[3], (1, STATE), jnp.float32, math.log(0.001), math.log(0.05)))
    observed = jnp.exp(jax.random.uniform(stochastic_seeds[5], (HORIZON_LENGTH, STATE), jnp.float32, math.log(0.001), math.log(0.004)))
    jitter = jnp.exp(jax.random.uniform(stochastic_seeds[4], (HORIZON_LENGTH, STATE), jnp.float32, math.log(0.5), math.log(2.0)))
    poisson_intensity = base_rate * jitter
    cluster_instant_tally = jax.random.randint(stochastic_seeds[6], (3,), 0, HORIZON_LENGTH)
    cluster_spans = jax.random.uniform(stochastic_seeds[7], (3,), jnp.float32, 0.5, 0.8)
    instant_locations = jnp.arange(HORIZON_LENGTH)
    cluster_members = jnp.prod(jnp.where(instant_locations[:, None] == cluster_instant_tally[None, :], cluster_spans[None, :], 1.0), axis=1)
    dynamics_transition = (1.0 - poisson_intensity) * cluster_members[:, None]
    identity = jnp.eye(STATE, dtype=jnp.float32)[None]
    precision = 0.5 * kernel + prec_diag[:, :, None] * identity
    return (precision, dynamics_transition, observed)


def draw_diag_blocks(key, part):
    precision, dynamics_transition, observed = smoother_parts(key)
    has_next = (jnp.arange(HORIZON_LENGTH) < HORIZON_LENGTH - 1).astype(jnp.float32)
    outer = dynamics_transition[:, :, None] * dynamics_transition[:, None, :]
    identity = jnp.eye(STATE, dtype=jnp.float32)[None]
    forward_term = has_next[:, None, None] * (outer * precision)
    return forward_term + jnp.roll(precision, 1, axis=0) + observed[:, :, None] * identity


def draw_coupling(key, part):
    precision, dynamics_transition, observed = smoother_parts(key)
    return -(dynamics_transition[:, :, None] * precision)


def draw_rhs(key, part):
    key_rough = jax.random.fold_in(jax.random.fold_in(key, 7), 0)
    return 0.04 * jax.random.truncated_normal(key_rough, -6.0, 6.0, (HORIZON_LENGTH, STATE), jnp.float32)


def setup_inputs(seed: int = 0) -> dict:
    keys = jax.random.split(jax.random.key(seed), 4)
    return {
        "diag_blocks": draw_diag_blocks(jax.random.fold_in(keys[3], 71), 0),
        "coupling": draw_coupling(jax.random.fold_in(keys[3], 71), 0),
        "rhs": draw_rhs(jax.random.fold_in(keys[3], 71), 0),
    }


def product(left_part, right_part):
    return jnp.dot(left_part, right_part, precision=lax.Precision.HIGHEST)

def cho_apply(factor, matrix):
    half_solved = lax.linalg.triangular_solve(factor, matrix, left_side=True, lower=True)
    return lax.linalg.triangular_solve(factor, half_solved, left_side=True, lower=True, transpose_a=True)

def reference(diag_blocks, coupling, rhs):
    step_count = diag_blocks.shape[0]
    state_width = diag_blocks.shape[1]
    instant_locations = jnp.arange(step_count)
    links_before = jnp.concatenate([jnp.zeros_like(coupling[:1]), coupling[:-1]], axis=0)
    links_after = coupling * (instant_locations < step_count - 1).astype(coupling.dtype)[:, None, None]

    def forward(carried, entries):
        factor_prev, vector_prev = carried
        diag_block, link_block, vector = entries
        solved = cho_apply(factor_prev, link_block)
        solved_vector = cho_apply(factor_prev, vector_prev[:, None])[:, 0]
        pivot_block = diag_block - product(link_block.T, solved)
        reduced = vector - product(link_block.T, solved_vector)
        factor = jnp.linalg.cholesky(pivot_block)
        log_det = 2.0 * jnp.sum(jnp.log(jnp.diagonal(factor)))
        return ((factor, reduced), (factor, reduced, log_det))
    start_carry = (jnp.eye(state_width, dtype=diag_blocks.dtype), jnp.zeros_like(rhs[0]))
    _, (factors, reduceds, log_dets) = lax.scan(forward, start_carry, (diag_blocks, links_before, rhs))

    def backward(next_state, entries):
        factor, reduced, link_block = entries
        now_state = cho_apply(factor, (reduced - product(link_block, next_state))[:, None])[:, 0]
        return (now_state, now_state)
    _, states = lax.scan(backward, jnp.zeros_like(rhs[0]), (factors, reduceds, links_after), reverse=True)
    logdet_mean = jnp.sum(log_dets) / (step_count * state_width)
    return (states, logdet_mean)
```

```python
import functools

import jax
import jax.numpy as jnp
from jax import lax
from jax.experimental import pallas as pl
from jax.experimental.pallas import tpu as pltpu
from jax.sharding import PartitionSpec as P

HIGHEST = lax.Precision.HIGHEST
TILE = 128
PANELS = 4


def dot(left, right, contract):
    return lax.dot_general(
        left, right, ((contract[0:1], contract[1:2]), ((), ())),
        precision=HIGHEST, preferred_element_type=jnp.float32,
    )


def sweep_tile(tiles):
    count = len(tiles)
    sub = lax.broadcasted_iota(jnp.int32, (8, TILE), 0)
    lane = lax.broadcasted_iota(jnp.int32, (8, TILE), 1)

    def row_of(value, j):
        return jnp.broadcast_to(value[j:j + 1, :], (8, TILE))

    def col_of(value, k):
        return jnp.broadcast_to(value[:, k:k + 1], (8, TILE))

    def one_panel(tiles, pivots, q):
        first = 8 * q
        in_panel = (lane >= first) & (lane < first + 8)
        minus_unit = jnp.where(lane - first == sub, -1.0, 0.0).astype(jnp.float32)
        panel = tiles[q]
        columns = [col_of(panel, first + m) for m in range(8)]
        swept = jnp.where(in_panel, minus_unit, panel)
        for j in range(8):
            pivot = row_of(columns[j], j)
            inverse = 1.0 / pivot
            pivots = jnp.where(lane == first + j, pivot, pivots)
            at_j = sub == j
            scale = jnp.where(at_j, -inverse, columns[j] * inverse)
            for m in range(j + 1, 8):
                columns[m] = jnp.where(at_j, 0.0, columns[m]) - scale * row_of(columns[m], j)
            swept = jnp.where(at_j, 0.0, swept) - scale * row_of(swept, j)
        rows = [row_of(swept, m) for m in range(8)]
        out = []
        for t in [(q + 1 + i) % count for i in range(count)]:
            if t == q:
                out.append((t, swept))
                continue
            parts = [col_of(tiles[t], first + m) * rows[m] for m in range(8)]
            while len(parts) > 1:
                parts = [a + b for a, b in zip(parts[::2], parts[1::2])]
            out.append((t, jnp.where(in_panel, 0.0, tiles[t]) - parts[0]))
        return [value for _, value in sorted(out, key=lambda pair: pair[0])], pivots

    def step(_, carry):
        tiles, pivots = list(carry[:-1]), carry[-1]
        for q in range(PANELS):
            tiles, pivots = one_panel(tiles, pivots, q)
        shift = TILE - 8 * PANELS
        tiles = tiles[PANELS:] + tiles[:PANELS]
        tiles = [pltpu.roll(value, shift, 1) for value in tiles]
        return (*tiles, pltpu.roll(pivots, shift, 1))

    ones = jnp.ones((8, TILE), jnp.float32)
    carry = lax.fori_loop(0, count // PANELS, step, (*tiles, ones))
    return list(carry[:-1]), carry[-1]


def inverse_kernel(size, matrix_ref, inverse_ref, logdet_ref, tile_ref, cols_ref):
    blocks = size // TILE
    inverse_ref[...] = matrix_ref[...]
    logdet_ref[...] = jnp.zeros((8, TILE), jnp.float32)

    @pl.loop(0, blocks)
    def _(block):
        start = pl.multiple_of(block * TILE, TILE)
        here = pl.ds(start, TILE)
        tiles = [
            inverse_ref[pl.ds(pl.multiple_of(start + 8 * t, 8), 8), here]
            for t in range(TILE // 8)
        ]
        tiles, pivots = sweep_tile(tiles)
        logdet_ref[...] += jnp.log(pivots)
        for t, value in enumerate(tiles):
            tile_ref[8 * t:8 * t + 8, :] = value
        cols_ref[...] = inverse_ref[:, here]
        cols_ref[here, :] = jnp.zeros((TILE, TILE), jnp.float32)
        inverse_ref[:, here] = jnp.zeros((size, TILE), jnp.float32)
        swept = -dot(tile_ref[...], inverse_ref[here, :], (1, 0))
        inverse_ref[here, :] = swept
        inverse_ref[here, here] = tile_ref[...]
        swept = inverse_ref[here, :]
        inverse_ref[...] -= dot(cols_ref[...], swept, (1, 0))

    inverse_ref[...] = -inverse_ref[...]


def inverted(matrix):
    size = matrix.shape[0]
    inverse, logs = pl.pallas_call(
        functools.partial(inverse_kernel, size),
        out_shape=(
            jax.ShapeDtypeStruct((size, size), jnp.float32),
            jax.ShapeDtypeStruct((8, TILE), jnp.float32),
        ),
        in_specs=[pl.BlockSpec(memory_space=pltpu.VMEM)],
        out_specs=(pl.BlockSpec(memory_space=pltpu.VMEM),) * 2,
        scratch_shapes=[
            pltpu.VMEM((TILE, TILE), jnp.float32),
            pltpu.VMEM((size, TILE), jnp.float32),
        ],
        compiler_params=pltpu.CompilerParams(vmem_limit_bytes=24 << 20),
        cost_estimate=pl.CostEstimate(
            flops=80 * size**3, bytes_accessed=8 * size * size, transcendentals=size
        ),
    )(matrix)
    return inverse, jnp.sum(logs[0])


def updates_kernel(rows, inverse_ref, left_ref, right_ref, both_ref, vector_ref, up_ref, down_ref):
    solved = dot(both_ref[...], inverse_ref[...], (1, 0))
    from_right = dot(solved, right_ref[...], (1, 0))
    up_ref[0:rows, :] = dot(solved[0:rows], left_ref[...], (1, 1))
    up_ref[rows:2 * rows, :] = -from_right[0:rows]
    down_ref[0:rows, :] = from_right[rows:]
    vector = dot(vector_ref[...], solved, (1, 1))
    up_ref[2 * rows:, :] = jnp.zeros_like(up_ref[2 * rows:, :])
    up_ref[2 * rows:, 0:rows] = vector[:, 0:rows]
    down_ref[rows:, :] = jnp.zeros_like(down_ref[rows:, :])
    down_ref[rows:, 0:rows] = vector[:, rows:]


def updates(inverse, left, right, left_rows, right_rows, vector):
    rows, size = left_rows.shape
    return pl.pallas_call(
        functools.partial(updates_kernel, rows),
        out_shape=(
            jax.ShapeDtypeStruct((2 * rows + 8, size), jnp.float32),
            jax.ShapeDtypeStruct((rows + 8, size), jnp.float32),
        ),
        in_specs=[pl.BlockSpec(memory_space=pltpu.VMEM)] * 5,
        out_specs=(pl.BlockSpec(memory_space=pltpu.VMEM),) * 2,
        compiler_params=pltpu.CompilerParams(vmem_limit_bytes=24 << 20),
    )(
        inverse, left, right, jnp.concatenate([left_rows, right_rows]),
        jnp.broadcast_to(vector[None], (8, size)),
    )


def product(left_part, right_part):
    return jnp.dot(left_part, right_part, precision=HIGHEST)


def shifted(block, axis, distance):
    devices = range(lax.axis_size(axis))
    route = [(i - distance, i) for i in devices if i - distance in devices]
    return lax.ppermute(block, axis, route)


def local(diag_blocks, coupling, rhs):
    group_steps, rows, size = diag_blocks.shape
    parts = lax.axis_size("rows")
    group_count = lax.axis_size("tm")
    group_index = lax.axis_index("tm")
    row_start = lax.axis_index("rows") * rows
    level_count = group_count.bit_length() - 1
    not_last = jnp.where(group_index == group_count - 1, 0.0, 1.0).astype(jnp.float32)

    def my_rows(matrix):
        return lax.dynamic_slice_in_dim(matrix, row_start, rows, 0)

    def my_columns_t(matrix):
        return lax.dynamic_slice_in_dim(matrix, row_start, rows, 1).T

    def gathered(packed):
        whole = lax.all_gather(packed, "rows", axis=0)
        diag = whole[:, :rows].reshape(size, size)
        link = whole[:, rows:2 * rows].reshape(size, size)
        vector = whole[:, 2 * rows, :rows].reshape(size)
        return diag, link, vector

    def as_row(vector):
        return jnp.pad(vector[None], ((0, 7), (0, size - rows)))

    right_rows_first = coupling[1] * not_last
    pivot = lax.all_gather(diag_blocks[1], "rows", axis=0, tiled=True)
    links = lax.all_gather(
        jnp.concatenate([coupling[0], right_rows_first, as_row(rhs[1])]), "rows", axis=0
    )
    left = links[:, :rows].reshape(size, size)
    right = links[:, rows:2 * rows].reshape(size, size)
    vector = links[:, 2 * rows, :rows].reshape(size)
    inverse, log_total = inverted(pivot)
    up, down = updates(inverse, left, right, coupling[0], my_columns_t(right), vector)
    chain = (inverse, left, right, vector)
    down = shifted(down, "tm", 1)
    packed = jnp.concatenate([
        diag_blocks[0] - up[:rows] - down[:rows],
        up[rows:2 * rows],
        as_row(rhs[0]) - up[2 * rows:] - down[rows:],
    ])
    levels_kept = []
    for level_index in range(level_count):
        stride = 1 << level_index
        is_pivot = group_index % (2 * stride) == stride
        survives = group_index % (2 * stride) == 0
        diag, right, vector = gathered(packed)
        left = shifted(right, "tm", stride)
        inverse, log_det = inverted(diag)
        up, down = updates(inverse, left, right, my_rows(left), my_columns_t(right), vector)
        levels_kept.append((is_pivot, inverse, left, right, vector))
        log_total = log_total + jnp.where(is_pivot, log_det, 0.0)
        up = shifted(up, "tm", -stride)
        down = shifted(down, "tm", stride)
        new = jnp.concatenate([
            packed[:rows] - up[:rows] - down[:rows],
            up[rows:2 * rows],
            packed[2 * rows:] - up[2 * rows:] - down[rows:],
        ])
        packed = jnp.where(survives, new, packed)
    diag, _, vector = gathered(packed)
    inverse, log_det = inverted(diag)
    log_total = log_total + jnp.where(group_index == 0, log_det, 0.0)
    total_det = lax.psum(log_total, "tm")
    states = product(inverse, vector)
    for level_index in reversed(range(level_count)):
        stride = 1 << level_index
        is_pivot, inverse, left, right, vector = levels_kept[level_index]
        below = shifted(states, "tm", stride)
        above = shifted(states, "tm", -stride)
        new_state = product(inverse, vector - product(below, left) - product(right, above))
        states = jnp.where(is_pivot, new_state, states)
    inverse, left, right, vector = chain
    following = shifted(states, "tm", -1)
    following = product(inverse, vector - product(states, left) - product(right, following))
    solution = jnp.stack([my_rows(states), my_rows(following)], axis=0)
    return (solution, total_det / (group_steps * group_count * size))


def solution(mesh):
    in_specs = (P("tm", "rows", None), P("tm", "rows", None), P("tm", "rows"))
    out_specs = (P("tm", "rows"), P())
    return jax.shard_map(local, mesh=mesh, in_specs=in_specs, out_specs=out_specs, check_vma=False)
```

```python
import functools

import jax
import jax.numpy as jnp
from jax import lax
from jax.experimental import pallas as pl
from jax.experimental.pallas import tpu as pltpu
from jax.sharding import PartitionSpec as P

HIGHEST = lax.Precision.HIGHEST
TILE = 128
PANELS = 4


def dot(left, right, contract):
    return lax.dot_general(
        left, right, ((contract[0:1], contract[1:2]), ((), ())),
        precision=HIGHEST, preferred_element_type=jnp.float32,
    )


def sweep_tile(tiles):
    count = len(tiles)
    sub = lax.broadcasted_iota(jnp.int32, (8, TILE), 0)
    lane = lax.broadcasted_iota(jnp.int32, (8, TILE), 1)

    def row_of(value, j):
        return jnp.broadcast_to(value[j:j + 1, :], (8, TILE))

    def col_of(value, k):
        return jnp.broadcast_to(value[:, k:k + 1], (8, TILE))

    def one_panel(tiles, pivots, q):
        first = 8 * q
        in_panel = (lane >= first) & (lane < first + 8)
        minus_unit = jnp.where(lane - first == sub, -1.0, 0.0).astype(jnp.float32)
        panel = tiles[q]
        columns = [col_of(panel, first + m) for m in range(8)]
        swept = jnp.where(in_panel, minus_unit, panel)
        for j in range(8):
            pivot = row_of(columns[j], j)
            inverse = 1.0 / pivot
            pivots = jnp.where(lane == first + j, pivot, pivots)
            at_j = sub == j
            scale = jnp.where(at_j, -inverse, columns[j] * inverse)
            for m in range(j + 1, 8):
                columns[m] = jnp.where(at_j, 0.0, columns[m]) - scale * row_of(columns[m], j)
            swept = jnp.where(at_j, 0.0, swept) - scale * row_of(swept, j)
        rows = [row_of(swept, m) for m in range(8)]
        out = []
        for t in [(q + 1 + i) % count for i in range(count)]:
            if t == q:
                out.append((t, swept))
                continue
            parts = [col_of(tiles[t], first + m) * rows[m] for m in range(8)]
            while len(parts) > 1:
                parts = [a + b for a, b in zip(parts[::2], parts[1::2])]
            out.append((t, jnp.where(in_panel, 0.0, tiles[t]) - parts[0]))
        return [value for _, value in sorted(out, key=lambda pair: pair[0])], pivots

    def step(_, carry):
        tiles, pivots = list(carry[:-1]), carry[-1]
        for q in range(PANELS):
            tiles, pivots = one_panel(tiles, pivots, q)
        shift = TILE - 8 * PANELS
        tiles = tiles[PANELS:] + tiles[:PANELS]
        tiles = [pltpu.roll(value, shift, 1) for value in tiles]
        return (*tiles, pltpu.roll(pivots, shift, 1))

    ones = jnp.ones((8, TILE), jnp.float32)
    carry = lax.fori_loop(0, count // PANELS, step, (*tiles, ones))
    return list(carry[:-1]), carry[-1]


def inverse_kernel(size, matrix_ref, inverse_ref, logdet_ref, tile_ref, cols_ref):
    blocks = size // TILE
    inverse_ref[...] = matrix_ref[...]
    logdet_ref[...] = jnp.zeros((8, TILE), jnp.float32)

    @pl.loop(0, blocks)
    def _(block):
        start = pl.multiple_of(block * TILE, TILE)
        here = pl.ds(start, TILE)
        tiles = [
            inverse_ref[pl.ds(pl.multiple_of(start + 8 * t, 8), 8), here]
            for t in range(TILE // 8)
        ]
        tiles, pivots = sweep_tile(tiles)
        logdet_ref[...] += jnp.log(pivots)
        for t, value in enumerate(tiles):
            tile_ref[8 * t:8 * t + 8, :] = value
        cols_ref[...] = inverse_ref[:, here]
        cols_ref[here, :] = jnp.zeros((TILE, TILE), jnp.float32)
        inverse_ref[:, here] = jnp.zeros((size, TILE), jnp.float32)
        swept = -dot(tile_ref[...], inverse_ref[here, :], (1, 0))
        inverse_ref[here, :] = swept
        inverse_ref[here, here] = tile_ref[...]
        swept = inverse_ref[here, :]
        inverse_ref[...] -= dot(cols_ref[...], swept, (1, 0))

    inverse_ref[...] = -inverse_ref[...]


def inverted(matrix):
    size = matrix.shape[0]
    inverse, logs = pl.pallas_call(
        functools.partial(inverse_kernel, size),
        out_shape=(
            jax.ShapeDtypeStruct((size, size), jnp.float32),
            jax.ShapeDtypeStruct((8, TILE), jnp.float32),
        ),
        in_specs=[pl.BlockSpec(memory_space=pltpu.VMEM)],
        out_specs=(pl.BlockSpec(memory_space=pltpu.VMEM),) * 2,
        scratch_shapes=[
            pltpu.VMEM((TILE, TILE), jnp.float32),
            pltpu.VMEM((size, TILE), jnp.float32),
        ],
        compiler_params=pltpu.CompilerParams(vmem_limit_bytes=24 << 20),
        cost_estimate=pl.CostEstimate(
            flops=80 * size**3, bytes_accessed=8 * size * size, transcendentals=size
        ),
    )(matrix)
    return inverse, logs


def updates_kernel(
    rows, inverse_ref, left_ref, right_ref, both_ref, vector_ref, logs_ref, tail_ref,
    up_ref, down_ref, link_ref,
):
    solved = dot(both_ref[...], inverse_ref[...], (1, 0))
    from_right = dot(solved, right_ref[...], (1, 0))
    up_ref[0:rows, :] = dot(solved[0:rows], left_ref[...], (1, 1))
    link_ref[...] = -from_right[0:rows]
    down_ref[0:rows, :] = from_right[rows:]
    vector = dot(vector_ref[...], solved, (1, 1))
    size = up_ref.shape[1]
    up_ref[rows:, :] = jnp.zeros((8, size), jnp.float32)
    up_ref[rows:, 0:rows] = vector[:, 0:rows]
    up_ref[rows:, size - TILE:] = logs_ref[...] - tail_ref[:, size - TILE:]
    down_ref[rows:, :] = jnp.zeros((8, size), jnp.float32)
    down_ref[rows:, 0:rows] = vector[:, rows:]


def updates(inverse, left, right, left_rows, right_rows, vector, logs, tail):
    rows, size = left_rows.shape
    message = jax.ShapeDtypeStruct((rows + 8, size), jnp.float32)
    return pl.pallas_call(
        functools.partial(updates_kernel, rows),
        out_shape=(message, message, jax.ShapeDtypeStruct((rows, size), jnp.float32)),
        in_specs=[pl.BlockSpec(memory_space=pltpu.VMEM)] * 7,
        out_specs=(pl.BlockSpec(memory_space=pltpu.VMEM),) * 3,
        compiler_params=pltpu.CompilerParams(vmem_limit_bytes=24 << 20),
    )(
        inverse, left, right, jnp.concatenate([left_rows, right_rows]),
        jnp.broadcast_to(vector[None], (8, size)), logs, tail,
    )


def product(left_part, right_part):
    return jnp.dot(left_part, right_part, precision=HIGHEST)


def shifted(block, axis, distance):
    devices = range(lax.axis_size(axis))
    route = [(i - distance, i) for i in devices if i - distance in devices]
    return lax.ppermute(block, axis, route)


def local(diag_blocks, coupling, rhs):
    group_steps, rows, size = diag_blocks.shape
    group_count = lax.axis_size("tm")
    group_index = lax.axis_index("tm")
    row_start = lax.axis_index("rows") * rows
    level_count = group_count.bit_length() - 1
    not_last = jnp.where(group_index == group_count - 1, 0.0, 1.0).astype(jnp.float32)

    def my_rows(matrix):
        return lax.dynamic_slice_in_dim(matrix, row_start, rows, 0)

    def my_columns_t(matrix):
        return lax.dynamic_slice_in_dim(matrix, row_start, rows, 1).T

    def gathered(part):
        return lax.all_gather(part, "rows", axis=0, tiled=True)

    def as_row(vector):
        return jnp.pad(vector[None], ((0, 7), (0, size - rows)))

    def eliminated(diag_part, left_part, right_part, vector_part, tail):
        diag = gathered(diag_part)
        left, right, vector = gathered(left_part), gathered(right_part), gathered(vector_part)
        inverse, logs = inverted(diag)
        up, down, link = updates(
            inverse, left, right, left_part, my_columns_t(right), vector, logs, tail
        )
        return up, down, link, (inverse, left, right, vector)

    tail = jnp.zeros((8, size), jnp.float32)
    up, down, link, chain = eliminated(
        diag_blocks[1], coupling[0], coupling[1] * not_last, rhs[1], tail
    )
    down = shifted(down, "tm", 1)
    left, right = shifted(link, "tm", 1), link
    diag = diag_blocks[0] - up[:rows] - down[:rows]
    tail = as_row(rhs[0]) - up[rows:] - down[rows:]
    levels_kept = []
    for level_index in range(level_count):
        stride = 1 << level_index
        is_pivot = group_index % (2 * stride) == stride
        up, down, link, kept = eliminated(diag, left, right, tail[0, :rows], tail)
        levels_kept.append((is_pivot, kept))
        up, down = shifted(up, "tm", -stride), shifted(down, "tm", stride)
        diag = diag - up[:rows] - down[:rows]
        tail = tail - up[rows:] - down[rows:]
        if level_index < level_count - 1:
            left, right = shifted(link, "tm", stride), shifted(link, "tm", -stride)
    vector = gathered(tail[0, :rows])
    inverse, logs = inverted(gathered(diag))
    total = jnp.sum(logs[0] - tail[0, size - TILE:])
    states = jnp.concatenate([product(inverse, vector), jnp.full((TILE,), total)])
    for level_index in reversed(range(level_count)):
        stride = 1 << level_index
        is_pivot, (inverse, left, right, vector) = levels_kept[level_index]
        below = shifted(states, "tm", stride)
        above = shifted(states, "tm", -stride)
        new_state = product(
            inverse, vector - product(below[:size], left) - product(right, above[:size])
        )
        states = jnp.where(is_pivot, jnp.concatenate([new_state, below[size:]]), states)
    total = states[size]
    states = states[:size]
    inverse, left, right, vector = chain
    following = shifted(states, "tm", -1)
    following = product(inverse, vector - product(states, left) - product(right, following))
    solution = jnp.stack([my_rows(states), my_rows(following)], axis=0)
    return (solution, total / (group_steps * group_count * size))


def solution(mesh):
    in_specs = (P("tm", "rows", None), P("tm", "rows", None), P("tm", "rows"))
    out_specs = (P("tm", "rows"), P())
    return jax.shard_map(local, mesh=mesh, in_specs=in_specs, out_specs=out_specs, check_vma=False)
```

```python
import functools

import jax
import jax.numpy as jnp
from jax import lax
from jax.experimental import pallas as pl
from jax.experimental.pallas import tpu as pltpu
from jax.sharding import PartitionSpec as P

HIGHEST = lax.Precision.HIGHEST
TILE = 128
PANELS = 4


def dot(left, right, contract):
    return lax.dot_general(
        left, right, ((contract[0:1], contract[1:2]), ((), ())),
        precision=HIGHEST, preferred_element_type=jnp.float32,
    )


def sweep_tile(tiles):
    count = len(tiles)
    sub = lax.broadcasted_iota(jnp.int32, (8, TILE), 0)
    lane = lax.broadcasted_iota(jnp.int32, (8, TILE), 1)

    def row_of(value, j):
        return jnp.broadcast_to(value[j:j + 1, :], (8, TILE))

    def col_of(value, k):
        return jnp.broadcast_to(value[:, k:k + 1], (8, TILE))

    def one_panel(tiles, pivots, q):
        first = 8 * q
        in_panel = (lane >= first) & (lane < first + 8)
        minus_unit = jnp.where(lane - first == sub, -1.0, 0.0).astype(jnp.float32)
        panel = tiles[q]
        columns = [col_of(panel, first + m) for m in range(8)]
        swept = jnp.where(in_panel, minus_unit, panel)
        for j in range(8):
            pivot = row_of(columns[j], j)
            inverse = 1.0 / pivot
            pivots = jnp.where(lane == first + j, pivot, pivots)
            at_j = sub == j
            scale = jnp.where(at_j, -inverse, columns[j] * inverse)
            for m in range(j + 1, 8):
                columns[m] = jnp.where(at_j, 0.0, columns[m]) - scale * row_of(columns[m], j)
            swept = jnp.where(at_j, 0.0, swept) - scale * row_of(swept, j)
        rows = [row_of(swept, m) for m in range(8)]
        out = []
        for t in [(q + 1 + i) % count for i in range(count)]:
            if t == q:
                out.append((t, swept))
                continue
            parts = [col_of(tiles[t], first + m) * rows[m] for m in range(8)]
            while len(parts) > 1:
                parts = [a + b for a, b in zip(parts[::2], parts[1::2])]
            out.append((t, jnp.where(in_panel, 0.0, tiles[t]) - parts[0]))
        return [value for _, value in sorted(out, key=lambda pair: pair[0])], pivots

    def step(_, carry):
        tiles, pivots = list(carry[:-1]), carry[-1]
        for q in range(PANELS):
            tiles, pivots = one_panel(tiles, pivots, q)
        shift = TILE - 8 * PANELS
        tiles = tiles[PANELS:] + tiles[:PANELS]
        tiles = [pltpu.roll(value, shift, 1) for value in tiles]
        return (*tiles, pltpu.roll(pivots, shift, 1))

    ones = jnp.ones((8, TILE), jnp.float32)
    carry = lax.fori_loop(0, count // PANELS, step, (*tiles, ones))
    return list(carry[:-1]), carry[-1]


def inverse_kernel(size, matrix_ref, inverse_ref, logdet_ref, tile_ref, cols_ref):
    blocks = size // TILE
    inverse_ref[...] = matrix_ref[...]
    logdet_ref[...] = jnp.zeros((8, TILE), jnp.float32)

    @pl.loop(0, blocks)
    def _(block):
        start = pl.multiple_of(block * TILE, TILE)
        here = pl.ds(start, TILE)
        tiles = [
            inverse_ref[pl.ds(pl.multiple_of(start + 8 * t, 8), 8), here]
            for t in range(TILE // 8)
        ]
        tiles, pivots = sweep_tile(tiles)
        logdet_ref[...] += jnp.log(pivots)
        for t, value in enumerate(tiles):
            tile_ref[8 * t:8 * t + 8, :] = value
        cols_ref[...] = inverse_ref[:, here]
        cols_ref[here, :] = jnp.zeros((TILE, TILE), jnp.float32)
        inverse_ref[:, here] = jnp.zeros((size, TILE), jnp.float32)
        swept = -dot(tile_ref[...], inverse_ref[here, :], (1, 0))
        inverse_ref[here, :] = swept
        inverse_ref[here, here] = tile_ref[...]
        swept = inverse_ref[here, :]
        inverse_ref[...] -= dot(cols_ref[...], swept, (1, 0))

    inverse_ref[...] = -inverse_ref[...]


def inverted(matrix):
    size = matrix.shape[0]
    inverse, logs = pl.pallas_call(
        functools.partial(inverse_kernel, size),
        out_shape=(
            jax.ShapeDtypeStruct((size, size), jnp.float32),
            jax.ShapeDtypeStruct((8, TILE), jnp.float32),
        ),
        in_specs=[pl.BlockSpec(memory_space=pltpu.VMEM)],
        out_specs=(pl.BlockSpec(memory_space=pltpu.VMEM),) * 2,
        scratch_shapes=[
            pltpu.VMEM((TILE, TILE), jnp.float32),
            pltpu.VMEM((size, TILE), jnp.float32),
        ],
        compiler_params=pltpu.CompilerParams(vmem_limit_bytes=24 << 20),
        cost_estimate=pl.CostEstimate(
            flops=80 * size**3, bytes_accessed=8 * size * size, transcendentals=size
        ),
    )(matrix)
    return inverse, logs


def updates_kernel(
    rows, inverse_ref, left_ref, right_ref, both_ref, vector_ref, logs_ref, tail_ref,
    up_ref, down_ref, link_ref,
):
    solved = dot(both_ref[...], inverse_ref[...], (1, 0))
    from_right = dot(solved, right_ref[...], (1, 0))
    up_ref[0:rows, :] = dot(solved[0:rows], left_ref[...], (1, 1))
    link_ref[...] = -from_right[0:rows]
    down_ref[0:rows, :] = from_right[rows:]
    vector = dot(vector_ref[...], solved, (1, 1))
    size = up_ref.shape[1]
    up_ref[rows:, :] = jnp.zeros((8, size), jnp.float32)
    up_ref[rows:, 0:rows] = vector[:, 0:rows]
    up_ref[rows:, size - TILE:] = logs_ref[...] - tail_ref[:, size - TILE:]
    down_ref[rows:, :] = jnp.zeros((8, size), jnp.float32)
    down_ref[rows:, 0:rows] = vector[:, rows:]


def updates(inverse, left, right, left_rows, right_rows, vector, logs, tail):
    rows, size = left_rows.shape
    message = jax.ShapeDtypeStruct((rows + 8, size), jnp.float32)
    return pl.pallas_call(
        functools.partial(updates_kernel, rows),
        out_shape=(message, message, jax.ShapeDtypeStruct((rows, size), jnp.float32)),
        in_specs=[pl.BlockSpec(memory_space=pltpu.VMEM)] * 7,
        out_specs=(pl.BlockSpec(memory_space=pltpu.VMEM),) * 3,
        compiler_params=pltpu.CompilerParams(vmem_limit_bytes=24 << 20),
    )(
        inverse, left, right, jnp.concatenate([left_rows, right_rows]),
        jnp.broadcast_to(vector[None], (8, size)), logs, tail,
    )


def exchange_kernel(
    stride, local_up, count, parts, own_ref, up_ref, down_ref, link_ref,
    new_ref, diag_ref, tails_ref, left_ref, right_ref,
    got_up, got_down, got_left, got_right, slots,
    send_sem, recv_sem, gather_send, gather_recv, forward_send, forward_recv,
):
    group, me = lax.axis_index("tm"), lax.axis_index("rows")
    rows = link_ref.shape[0]
    below = lax.rem(group + count - stride, count)
    above = lax.rem(group + stride, count)
    partner = me + 1 - 2 * lax.rem(me, 2)

    barrier = pltpu.get_barrier_semaphore()
    for other in (below, above):
        pl.semaphore_signal(
            barrier, inc=1, device_id={"tm": other}, device_id_type=pl.DeviceIdType.MESH
        )
    for distance in range(1, parts):
        pl.semaphore_signal(
            barrier, inc=1, device_id={"rows": lax.rem(me + distance, parts)},
            device_id_type=pl.DeviceIdType.MESH,
        )
    pl.semaphore_wait(barrier, parts + 1)

    if local_up:
        sends_down, gets_down = group < count - 1, group > 0
    else:
        place = lax.rem(group, 2 * stride)
        gets_up, sends_up = place == 0, place == stride
        sends_down = jnp.logical_and(place == stride, group + stride < count)
        gets_down = jnp.logical_and(place == 0, group > 0)

    def over_time(source, target, number, other):
        return pltpu.make_async_remote_copy(
            src_ref=source, dst_ref=target, send_sem=send_sem.at[number],
            recv_sem=recv_sem.at[number], device_id={"tm": other},
            device_id_type=pl.DeviceIdType.MESH,
        )

    up = over_time(up_ref, got_up, 0, below)
    down = over_time(down_ref, got_down, 1, above)
    link_up = over_time(link_ref, got_right, 2, below)
    link_down = over_time(link_ref, got_left, 3, above)

    if not local_up:
        @pl.when(sends_up)
        def _():
            up.start()

    @pl.when(sends_down)
    def _():
        down.start()

    if not local_up:
        @pl.when(sends_up)
        def _():
            link_up.start()

    @pl.when(sends_down)
    def _():
        link_down.start()

    if local_up:
        new_ref[...] = own_ref[...] - up_ref[...]
    else:
        new_ref[...] = own_ref[...]

        @pl.when(gets_up)
        def _():
            up.wait_recv()
            new_ref[...] -= got_up[...]

    @pl.when(gets_down)
    def _():
        down.wait_recv()
        new_ref[...] -= got_down[...]

    def over_rows(source, slot, target, send, recv):
        return pltpu.make_async_remote_copy(
            src_ref=source, dst_ref=slots.at[slot], send_sem=send, recv_sem=recv,
            device_id={"rows": target}, device_id_type=pl.DeviceIdType.MESH,
        )

    chips = parts // 2
    sent = []
    for d in range(1, chips):
        target = lax.rem(me + 2 * d, parts)
        copy = over_rows(new_ref, me, target, gather_send.at[d], gather_recv.at[d])
        copy.start()
        sent.append(copy)
    forwards = [over_rows(new_ref, me, partner, forward_send.at[0], forward_recv.at[0])]
    forwards[0].start()
    slots[me] = new_ref[...]
    for d in range(1, chips):
        sent[d - 1].wait_recv()
        source = lax.rem(me + parts - 2 * d, parts)
        copy = over_rows(
            slots.at[source], source, partner, forward_send.at[d], forward_recv.at[d]
        )
        copy.start()
        forwards.append(copy)
    for copy in forwards:
        copy.wait_recv()
    for copy in sent + forwards:
        copy.wait_send()
    for part in range(parts):
        diag_ref[part * rows:(part + 1) * rows, :] = slots[part, 0:rows, :]
        tails_ref[part * 8:(part + 1) * 8, :] = slots[part, rows:, :]

    left_ref[...] = jnp.zeros(left_ref.shape, jnp.float32)

    @pl.when(gets_down)
    def _():
        link_down.wait_recv()
        left_ref[...] = got_left[...]

    if local_up:
        right_ref[...] = link_ref[...]
    else:
        right_ref[...] = jnp.zeros(right_ref.shape, jnp.float32)

        @pl.when(gets_up)
        def _():
            link_up.wait_recv()
            right_ref[...] = got_right[...]

        @pl.when(sends_up)
        def _():
            up.wait_send()
            link_up.wait_send()

    @pl.when(sends_down)
    def _():
        down.wait_send()
        link_down.wait_send()


def exchanged(number, stride, local_up, own, up, down, link):
    rows, size = link.shape
    count, parts = lax.axis_size("tm"), lax.axis_size("rows")
    message = jax.ShapeDtypeStruct((rows + 8, size), jnp.float32)
    part = jax.ShapeDtypeStruct((rows, size), jnp.float32)
    new, diag, tails, left, right = pl.pallas_call(
        functools.partial(exchange_kernel, stride, local_up, count, parts),
        out_shape=(
            message, jax.ShapeDtypeStruct((size, size), jnp.float32),
            jax.ShapeDtypeStruct((8 * parts, size), jnp.float32), part, part,
        ),
        in_specs=[pl.BlockSpec(memory_space=pltpu.VMEM)] * 4,
        out_specs=(pl.BlockSpec(memory_space=pltpu.VMEM),) * 5,
        scratch_shapes=[
            pltpu.VMEM((rows + 8, size), jnp.float32),
            pltpu.VMEM((rows + 8, size), jnp.float32),
            pltpu.VMEM((rows, size), jnp.float32),
            pltpu.VMEM((rows, size), jnp.float32),
            pltpu.VMEM((parts, rows + 8, size), jnp.float32),
            pltpu.SemaphoreType.DMA((4,)),
            pltpu.SemaphoreType.DMA((4,)),
            pltpu.SemaphoreType.DMA((parts // 2,)),
            pltpu.SemaphoreType.DMA((parts // 2,)),
            pltpu.SemaphoreType.DMA((parts // 2,)),
            pltpu.SemaphoreType.DMA((parts // 2,)),
        ],
        compiler_params=pltpu.CompilerParams(
            collective_id=number, has_side_effects=True, vmem_limit_bytes=24 << 20
        ),
    )(own, up, down, link)
    vector = tails.reshape(parts, 8, size)[:, 0, :rows].reshape(size)
    return new, diag, vector, left, right


def product(left_part, right_part):
    return jnp.dot(left_part, right_part, precision=HIGHEST)


def shifted(block, axis, distance):
    devices = range(lax.axis_size(axis))
    route = [(i - distance, i) for i in devices if i - distance in devices]
    return lax.ppermute(block, axis, route)


def local(diag_blocks, coupling, rhs):
    group_steps, rows, size = diag_blocks.shape
    group_count = lax.axis_size("tm")
    group_index = lax.axis_index("tm")
    row_start = lax.axis_index("rows") * rows
    level_count = group_count.bit_length() - 1
    not_last = jnp.where(group_index == group_count - 1, 0.0, 1.0).astype(jnp.float32)

    def my_rows(matrix):
        return lax.dynamic_slice_in_dim(matrix, row_start, rows, 0)

    def my_columns_t(matrix):
        return lax.dynamic_slice_in_dim(matrix, row_start, rows, 1).T

    def gathered(part):
        return lax.all_gather(part, "rows", axis=0, tiled=True)

    def as_row(vector):
        return jnp.pad(vector[None], ((0, 7), (0, size - rows)))

    def eliminated(diag, vector, left_part, right_part, tail):
        left, right = gathered(left_part), gathered(right_part)
        inverse, logs = inverted(diag)
        up, down, link = updates(
            inverse, left, right, left_part, my_columns_t(right), vector, logs, tail
        )
        return up, down, link, (inverse, left, right, vector)

    up, down, link, chain = eliminated(
        gathered(diag_blocks[1]), gathered(rhs[1]), coupling[0], coupling[1] * not_last,
        jnp.zeros((8, size), jnp.float32),
    )
    own = jnp.concatenate([diag_blocks[0], as_row(rhs[0])])
    own, diag, vector, left, right = exchanged(0, 1, True, own, up, down, link)
    levels_kept = []
    for level_index in range(level_count):
        stride = 1 << level_index
        is_pivot = group_index % (2 * stride) == stride
        up, down, link, kept = eliminated(diag, vector, left, right, own[rows:])
        levels_kept.append((is_pivot, kept))
        own, diag, vector, left, right = exchanged(
            level_index + 1, stride, False, own, up, down, link
        )
    tail = own[rows:]
    inverse, logs = inverted(diag)
    total = jnp.sum(logs[0] - tail[0, size - TILE:])
    states = jnp.concatenate([product(inverse, vector), jnp.full((TILE,), total)])
    for level_index in reversed(range(level_count)):
        stride = 1 << level_index
        is_pivot, (inverse, left, right, vector) = levels_kept[level_index]
        below = shifted(states, "tm", stride)
        above = shifted(states, "tm", -stride)
        new_state = product(
            inverse, vector - product(below[:size], left) - product(right, above[:size])
        )
        states = jnp.where(is_pivot, jnp.concatenate([new_state, below[size:]]), states)
    total = states[size]
    states = states[:size]
    inverse, left, right, vector = chain
    following = shifted(states, "tm", -1)
    following = product(inverse, vector - product(states, left) - product(right, following))
    solution = jnp.stack([my_rows(states), my_rows(following)], axis=0)
    return (solution, total / (group_steps * group_count * size))


def solution(mesh):
    in_specs = (P("tm", "rows", None), P("tm", "rows", None), P("tm", "rows"))
    out_specs = (P("tm", "rows"), P())
    return jax.shard_map(local, mesh=mesh, in_specs=in_specs, out_specs=out_specs, check_vma=False)
```

```python
import functools

import jax
import jax.numpy as jnp
from jax import lax
from jax.experimental import pallas as pl
from jax.experimental.pallas import tpu as pltpu
from jax.sharding import PartitionSpec as P

HIGHEST = lax.Precision.HIGHEST
TILE = 128
PANELS = 4


def dot(left, right, contract):
    return lax.dot_general(
        left, right, ((contract[0:1], contract[1:2]), ((), ())),
        precision=HIGHEST, preferred_element_type=jnp.float32,
    )


def sweep_tile(tiles):
    count = len(tiles)
    sub = lax.broadcasted_iota(jnp.int32, (8, TILE), 0)
    lane = lax.broadcasted_iota(jnp.int32, (8, TILE), 1)

    def row_of(value, j):
        return jnp.broadcast_to(value[j:j + 1, :], (8, TILE))

    def col_of(value, k):
        return jnp.broadcast_to(value[:, k:k + 1], (8, TILE))

    def one_panel(tiles, pivots, q):
        first = 8 * q
        in_panel = (lane >= first) & (lane < first + 8)
        minus_unit = jnp.where(lane - first == sub, -1.0, 0.0).astype(jnp.float32)
        panel = tiles[q]
        columns = [col_of(panel, first + m) for m in range(8)]
        swept = jnp.where(in_panel, minus_unit, panel)
        for j in range(8):
            pivot = row_of(columns[j], j)
            inverse = 1.0 / pivot
            pivots = jnp.where(lane == first + j, pivot, pivots)
            at_j = sub == j
            scale = jnp.where(at_j, -inverse, columns[j] * inverse)
            for m in range(j + 1, 8):
                columns[m] = jnp.where(at_j, 0.0, columns[m]) - scale * row_of(columns[m], j)
            swept = jnp.where(at_j, 0.0, swept) - scale * row_of(swept, j)
        rows = [row_of(swept, m) for m in range(8)]
        out = []
        for t in [(q + 1 + i) % count for i in range(count)]:
            if t == q:
                out.append((t, swept))
                continue
            parts = [col_of(tiles[t], first + m) * rows[m] for m in range(8)]
            while len(parts) > 1:
                parts = [a + b for a, b in zip(parts[::2], parts[1::2])]
            out.append((t, jnp.where(in_panel, 0.0, tiles[t]) - parts[0]))
        return [value for _, value in sorted(out, key=lambda pair: pair[0])], pivots

    def step(_, carry):
        tiles, pivots = list(carry[:-1]), carry[-1]
        for q in range(PANELS):
            tiles, pivots = one_panel(tiles, pivots, q)
        shift = TILE - 8 * PANELS
        tiles = tiles[PANELS:] + tiles[:PANELS]
        tiles = [pltpu.roll(value, shift, 1) for value in tiles]
        return (*tiles, pltpu.roll(pivots, shift, 1))

    ones = jnp.ones((8, TILE), jnp.float32)
    carry = lax.fori_loop(0, count // PANELS, step, (*tiles, ones))
    return list(carry[:-1]), carry[-1]


def inverse_kernel(size, matrix_ref, inverse_ref, logdet_ref, tile_ref, cols_ref):
    blocks = size // TILE
    inverse_ref[...] = matrix_ref[...]
    logdet_ref[...] = jnp.zeros((8, TILE), jnp.float32)

    @pl.loop(0, blocks)
    def _(block):
        start = pl.multiple_of(block * TILE, TILE)
        here = pl.ds(start, TILE)
        tiles = [
            inverse_ref[pl.ds(pl.multiple_of(start + 8 * t, 8), 8), here]
            for t in range(TILE // 8)
        ]
        tiles, pivots = sweep_tile(tiles)
        logdet_ref[...] += jnp.log(pivots)
        for t, value in enumerate(tiles):
            tile_ref[8 * t:8 * t + 8, :] = value
        cols_ref[...] = inverse_ref[:, here]
        cols_ref[here, :] = jnp.zeros((TILE, TILE), jnp.float32)
        inverse_ref[:, here] = jnp.zeros((size, TILE), jnp.float32)
        swept = -dot(tile_ref[...], inverse_ref[here, :], (1, 0))
        inverse_ref[here, :] = swept
        inverse_ref[here, here] = tile_ref[...]
        swept = inverse_ref[here, :]
        inverse_ref[...] -= dot(cols_ref[...], swept, (1, 0))

    inverse_ref[...] = -inverse_ref[...]


def inverted(matrix):
    size = matrix.shape[0]
    inverse, logs = pl.pallas_call(
        functools.partial(inverse_kernel, size),
        out_shape=(
            jax.ShapeDtypeStruct((size, size), jnp.float32),
            jax.ShapeDtypeStruct((8, TILE), jnp.float32),
        ),
        in_specs=[pl.BlockSpec(memory_space=pltpu.VMEM)],
        out_specs=(pl.BlockSpec(memory_space=pltpu.VMEM),) * 2,
        scratch_shapes=[
            pltpu.VMEM((TILE, TILE), jnp.float32),
            pltpu.VMEM((size, TILE), jnp.float32),
        ],
        compiler_params=pltpu.CompilerParams(vmem_limit_bytes=24 << 20),
        cost_estimate=pl.CostEstimate(
            flops=80 * size**3, bytes_accessed=8 * size * size, transcendentals=size
        ),
    )(matrix)
    return inverse, logs


def updates_kernel(
    rows, inverse_ref, left_ref, right_ref, left_rows_ref, right_rows_ref, vector_ref,
    logs_ref, tail_ref, up_ref, down_ref, link_ref,
):
    both = jnp.concatenate([left_rows_ref[...], right_rows_ref[...]])
    solved = dot(both, inverse_ref[...], (1, 0))
    from_right = dot(solved, right_ref[...], (1, 0))
    up_ref[0:rows, :] = dot(solved[0:rows], left_ref[...], (1, 1))
    link_ref[...] = -from_right[0:rows]
    down_ref[0:rows, :] = from_right[rows:]
    vector = dot(vector_ref[...], solved, (1, 1))
    size = up_ref.shape[1]
    up_ref[rows:, :] = jnp.zeros((8, size), jnp.float32)
    up_ref[rows:, 0:rows] = vector[:, 0:rows]
    up_ref[rows:, size - TILE:] = logs_ref[...] - tail_ref[:, size - TILE:]
    down_ref[rows:, :] = jnp.zeros((8, size), jnp.float32)
    down_ref[rows:, 0:rows] = vector[:, rows:]


def updates(inverse, left, right, left_rows, right_rows, vector, logs, tail):
    rows, size = left_rows.shape
    message = jax.ShapeDtypeStruct((rows + 8, size), jnp.float32)
    return pl.pallas_call(
        functools.partial(updates_kernel, rows),
        out_shape=(message, message, jax.ShapeDtypeStruct((rows, size), jnp.float32)),
        in_specs=[pl.BlockSpec(memory_space=pltpu.VMEM)] * 8,
        out_specs=(pl.BlockSpec(memory_space=pltpu.VMEM),) * 3,
        compiler_params=pltpu.CompilerParams(vmem_limit_bytes=24 << 20),
    )(
        inverse, left, right, left_rows, right_rows,
        jnp.broadcast_to(vector[None], (8, size)), logs, tail,
    )


def exchange_kernel(
    stride, local_up, count, parts, own_ref, up_ref, down_ref, link_ref,
    new_ref, diag_ref, tails_ref, left_ref, right_ref,
    got_up, got_down, got_left, got_right, slots,
    send_sem, recv_sem, gather_send, gather_recv, forward_send, forward_recv,
):
    group, me = lax.axis_index("tm"), lax.axis_index("rows")
    rows = link_ref.shape[0]
    below = lax.rem(group + count - stride, count)
    above = lax.rem(group + stride, count)
    partner = me + 1 - 2 * lax.rem(me, 2)

    barrier = pltpu.get_barrier_semaphore()
    for other in (below, above):
        pl.semaphore_signal(
            barrier, inc=1, device_id={"tm": other}, device_id_type=pl.DeviceIdType.MESH
        )
    for distance in range(1, parts):
        pl.semaphore_signal(
            barrier, inc=1, device_id={"rows": lax.rem(me + distance, parts)},
            device_id_type=pl.DeviceIdType.MESH,
        )
    pl.semaphore_wait(barrier, parts + 1)

    if local_up:
        sends_down, gets_down = group < count - 1, group > 0
    else:
        place = lax.rem(group, 2 * stride)
        gets_up, sends_up = place == 0, place == stride
        sends_down = jnp.logical_and(place == stride, group + stride < count)
        gets_down = jnp.logical_and(place == 0, group > 0)

    def over_time(source, target, number, other):
        return pltpu.make_async_remote_copy(
            src_ref=source, dst_ref=target, send_sem=send_sem.at[number],
            recv_sem=recv_sem.at[number], device_id={"tm": other},
            device_id_type=pl.DeviceIdType.MESH,
        )

    up = over_time(up_ref, got_up, 0, below)
    down = over_time(down_ref, got_down, 1, above)
    link_up = over_time(link_ref, got_right, 2, below)
    link_down = over_time(link_ref, got_left, 3, above)

    if not local_up:
        @pl.when(sends_up)
        def _():
            up.start()

    @pl.when(sends_down)
    def _():
        down.start()

    if not local_up:
        @pl.when(sends_up)
        def _():
            link_up.start()

    @pl.when(sends_down)
    def _():
        link_down.start()

    if local_up:
        new_ref[...] = own_ref[...] - up_ref[...]
    else:
        new_ref[...] = own_ref[...]

        @pl.when(gets_up)
        def _():
            up.wait_recv()
            new_ref[...] -= got_up[...]

    @pl.when(gets_down)
    def _():
        down.wait_recv()
        new_ref[...] -= got_down[...]

    def over_rows(source, slot, target, send, recv):
        return pltpu.make_async_remote_copy(
            src_ref=source, dst_ref=slots.at[slot], send_sem=send, recv_sem=recv,
            device_id={"rows": target}, device_id_type=pl.DeviceIdType.MESH,
        )

    chips = parts // 2
    sent = []
    for d in range(1, chips):
        target = lax.rem(me + 2 * d, parts)
        copy = over_rows(new_ref, me, target, gather_send.at[d], gather_recv.at[d])
        copy.start()
        sent.append(copy)
    forwards = [over_rows(new_ref, me, partner, forward_send.at[0], forward_recv.at[0])]
    forwards[0].start()
    slots[me] = new_ref[...]
    for d in range(1, chips):
        sent[d - 1].wait_recv()
        source = lax.rem(me + parts - 2 * d, parts)
        copy = over_rows(
            slots.at[source], source, partner, forward_send.at[d], forward_recv.at[d]
        )
        copy.start()
        forwards.append(copy)
    for copy in forwards:
        copy.wait_recv()
    for copy in sent + forwards:
        copy.wait_send()
    for part in range(parts):
        diag_ref[part * rows:(part + 1) * rows, :] = slots[part, 0:rows, :]
        tails_ref[part * 8:(part + 1) * 8, :] = slots[part, rows:, :]

    left_ref[...] = jnp.zeros(left_ref.shape, jnp.float32)

    @pl.when(gets_down)
    def _():
        link_down.wait_recv()
        left_ref[...] = got_left[...]

    if local_up:
        right_ref[...] = link_ref[...]
    else:
        right_ref[...] = jnp.zeros(right_ref.shape, jnp.float32)

        @pl.when(gets_up)
        def _():
            link_up.wait_recv()
            right_ref[...] = got_right[...]

        @pl.when(sends_up)
        def _():
            up.wait_send()
            link_up.wait_send()

    @pl.when(sends_down)
    def _():
        down.wait_send()
        link_down.wait_send()


def exchanged(number, stride, local_up, own, up, down, link):
    rows, size = link.shape
    count, parts = lax.axis_size("tm"), lax.axis_size("rows")
    message = jax.ShapeDtypeStruct((rows + 8, size), jnp.float32)
    part = jax.ShapeDtypeStruct((rows, size), jnp.float32)
    new, diag, tails, left, right = pl.pallas_call(
        functools.partial(exchange_kernel, stride, local_up, count, parts),
        out_shape=(
            message, jax.ShapeDtypeStruct((size, size), jnp.float32),
            jax.ShapeDtypeStruct((8 * parts, size), jnp.float32), part, part,
        ),
        in_specs=[pl.BlockSpec(memory_space=pltpu.VMEM)] * 4,
        out_specs=(pl.BlockSpec(memory_space=pltpu.VMEM),) * 5,
        scratch_shapes=[
            pltpu.VMEM((rows + 8, size), jnp.float32),
            pltpu.VMEM((rows + 8, size), jnp.float32),
            pltpu.VMEM((rows, size), jnp.float32),
            pltpu.VMEM((rows, size), jnp.float32),
            pltpu.VMEM((parts, rows + 8, size), jnp.float32),
            pltpu.SemaphoreType.DMA((4,)),
            pltpu.SemaphoreType.DMA((4,)),
            pltpu.SemaphoreType.DMA((parts // 2,)),
            pltpu.SemaphoreType.DMA((parts // 2,)),
            pltpu.SemaphoreType.DMA((parts // 2,)),
            pltpu.SemaphoreType.DMA((parts // 2,)),
        ],
        compiler_params=pltpu.CompilerParams(
            collective_id=number, has_side_effects=True, vmem_limit_bytes=24 << 20
        ),
    )(own, up, down, link)
    vector = tails.reshape(parts, 8, size)[:, 0, :rows].reshape(size)
    return new, diag, vector, left, right


def product(left_part, right_part):
    return jnp.dot(left_part, right_part, precision=HIGHEST)


def shifted(block, axis, distance):
    devices = range(lax.axis_size(axis))
    route = [(i - distance, i) for i in devices if i - distance in devices]
    return lax.ppermute(block, axis, route)


def local(diag_blocks, coupling, rhs):
    group_steps, rows, size = diag_blocks.shape
    group_count = lax.axis_size("tm")
    group_index = lax.axis_index("tm")
    row_start = lax.axis_index("rows") * rows
    level_count = group_count.bit_length() - 1
    not_last = jnp.where(group_index == group_count - 1, 0.0, 1.0).astype(jnp.float32)

    def my_rows(matrix):
        return lax.dynamic_slice_in_dim(matrix, row_start, rows, 0)

    def my_columns_t(matrix):
        return lax.dynamic_slice_in_dim(matrix, row_start, rows, 1).T

    def gathered(part):
        return lax.all_gather(part, "rows", axis=0, tiled=True)

    def as_row(vector):
        return jnp.pad(vector[None], ((0, 7), (0, size - rows)))

    def eliminated(diag, vector, left_part, right_part, tail):
        left, right = gathered(left_part), gathered(right_part)
        inverse, logs = inverted(diag)
        up, down, link = updates(
            inverse, left, right, left_part, my_columns_t(right), vector, logs, tail
        )
        return up, down, link, (inverse, left, right, vector)

    pivot, left, right, vector = lax.optimization_barrier((
        gathered(diag_blocks[1]), coupling[0], coupling[1] * not_last, as_row(rhs[1])
    ))
    vector = gathered(vector).reshape(-1, 8, size)[:, 0, :rows].reshape(size)
    up, down, link, chain = eliminated(
        pivot, vector, left, right, jnp.zeros((8, size), jnp.float32)
    )
    own = jnp.concatenate([diag_blocks[0], as_row(rhs[0])])
    own, diag, vector, left, right = exchanged(0, 1, True, own, up, down, link)
    levels_kept = []
    for level_index in range(level_count):
        stride = 1 << level_index
        is_pivot = group_index % (2 * stride) == stride
        up, down, link, kept = eliminated(diag, vector, left, right, own[rows:])
        levels_kept.append((is_pivot, kept))
        own, diag, vector, left, right = exchanged(
            level_index + 1, stride, False, own, up, down, link
        )
    tail = own[rows:]
    inverse, logs = inverted(diag)
    total = jnp.sum(logs[0] - tail[0, size - TILE:])
    states = jnp.concatenate([product(inverse, vector), jnp.full((TILE,), total)])
    for level_index in reversed(range(level_count)):
        stride = 1 << level_index
        is_pivot, (inverse, left, right, vector) = levels_kept[level_index]
        below = shifted(states, "tm", stride)
        above = shifted(states, "tm", -stride)
        new_state = product(
            inverse, vector - product(below[:size], left) - product(right, above[:size])
        )
        states = jnp.where(is_pivot, jnp.concatenate([new_state, below[size:]]), states)
    total = states[size]
    states = states[:size]
    inverse, left, right, vector = chain
    following = shifted(states, "tm", -1)
    following = product(inverse, vector - product(states, left) - product(right, following))
    solution = jnp.stack([my_rows(states), my_rows(following)], axis=0)
    return (solution, total / (group_steps * group_count * size))


def solution(mesh):
    in_specs = (P("tm", "rows", None), P("tm", "rows", None), P("tm", "rows"))
    out_specs = (P("tm", "rows"), P())
    return jax.shard_map(local, mesh=mesh, in_specs=in_specs, out_specs=out_specs, check_vma=False)
```

```python
import functools

import jax
import jax.numpy as jnp
from jax import lax
from jax.experimental import pallas as pl
from jax.experimental.pallas import tpu as pltpu
from jax.sharding import PartitionSpec as P

HIGHEST = lax.Precision.HIGHEST
TILE = 128
PANELS = 4


def dot(left, right, contract):
    return lax.dot_general(
        left, right, ((contract[0:1], contract[1:2]), ((), ())),
        precision=HIGHEST, preferred_element_type=jnp.float32,
    )


def sweep_tile(tiles):
    count = len(tiles)
    sub = lax.broadcasted_iota(jnp.int32, (8, TILE), 0)
    lane = lax.broadcasted_iota(jnp.int32, (8, TILE), 1)

    def row_of(value, j):
        return jnp.broadcast_to(value[j:j + 1, :], (8, TILE))

    def col_of(value, k):
        return jnp.broadcast_to(value[:, k:k + 1], (8, TILE))

    def one_panel(tiles, pivots, q):
        first = 8 * q
        in_panel = (lane >= first) & (lane < first + 8)
        minus_unit = jnp.where(lane - first == sub, -1.0, 0.0).astype(jnp.float32)
        panel = tiles[q]
        columns = [col_of(panel, first + m) for m in range(8)]
        swept = jnp.where(in_panel, minus_unit, panel)
        for j in range(8):
            pivot = row_of(columns[j], j)
            inverse = 1.0 / pivot
            pivots = jnp.where(lane == first + j, pivot, pivots)
            at_j = sub == j
            scale = jnp.where(at_j, -inverse, columns[j] * inverse)
            for m in range(j + 1, 8):
                columns[m] = jnp.where(at_j, 0.0, columns[m]) - scale * row_of(columns[m], j)
            swept = jnp.where(at_j, 0.0, swept) - scale * row_of(swept, j)
        rows = [row_of(swept, m) for m in range(8)]
        out = []
        for t in [(q + 1 + i) % count for i in range(count)]:
            if t == q:
                out.append((t, swept))
                continue
            parts = [col_of(tiles[t], first + m) * rows[m] for m in range(8)]
            while len(parts) > 1:
                parts = [a + b for a, b in zip(parts[::2], parts[1::2])]
            out.append((t, jnp.where(in_panel, 0.0, tiles[t]) - parts[0]))
        return [value for _, value in sorted(out, key=lambda pair: pair[0])], pivots

    def step(_, carry):
        tiles, pivots = list(carry[:-1]), carry[-1]
        for q in range(PANELS):
            tiles, pivots = one_panel(tiles, pivots, q)
        shift = TILE - 8 * PANELS
        tiles = tiles[PANELS:] + tiles[:PANELS]
        tiles = [pltpu.roll(value, shift, 1) for value in tiles]
        return (*tiles, pltpu.roll(pivots, shift, 1))

    ones = jnp.ones((8, TILE), jnp.float32)
    carry = lax.fori_loop(0, count // PANELS, step, (*tiles, ones))
    return list(carry[:-1]), carry[-1]


def inverse_kernel(size, matrix_ref, inverse_ref, logdet_ref, tile_ref, cols_ref):
    blocks = size // TILE
    inverse_ref[...] = matrix_ref[...]
    logdet_ref[...] = jnp.zeros((8, TILE), jnp.float32)

    @pl.loop(0, blocks)
    def _(block):
        start = pl.multiple_of(block * TILE, TILE)
        here = pl.ds(start, TILE)
        tiles = [
            inverse_ref[pl.ds(pl.multiple_of(start + 8 * t, 8), 8), here]
            for t in range(TILE // 8)
        ]
        tiles, pivots = sweep_tile(tiles)
        logdet_ref[...] += jnp.log(pivots)
        for t, value in enumerate(tiles):
            tile_ref[8 * t:8 * t + 8, :] = value
        cols_ref[...] = inverse_ref[:, here]
        cols_ref[here, :] = jnp.zeros((TILE, TILE), jnp.float32)
        inverse_ref[:, here] = jnp.zeros((size, TILE), jnp.float32)
        swept = -dot(tile_ref[...], inverse_ref[here, :], (1, 0))
        inverse_ref[here, :] = swept
        inverse_ref[here, here] = tile_ref[...]
        swept = inverse_ref[here, :]
        inverse_ref[...] -= dot(cols_ref[...], swept, (1, 0))

    inverse_ref[...] = -inverse_ref[...]


def inverted(matrix):
    size = matrix.shape[0]
    inverse, logs = pl.pallas_call(
        functools.partial(inverse_kernel, size),
        out_shape=(
            jax.ShapeDtypeStruct((size, size), jnp.float32),
            jax.ShapeDtypeStruct((8, TILE), jnp.float32),
        ),
        in_specs=[pl.BlockSpec(memory_space=pltpu.VMEM)],
        out_specs=(pl.BlockSpec(memory_space=pltpu.VMEM),) * 2,
        scratch_shapes=[
            pltpu.VMEM((TILE, TILE), jnp.float32),
            pltpu.VMEM((size, TILE), jnp.float32),
        ],
        compiler_params=pltpu.CompilerParams(vmem_limit_bytes=24 << 20),
        cost_estimate=pl.CostEstimate(
            flops=80 * size**3, bytes_accessed=8 * size * size, transcendentals=size
        ),
    )(matrix)
    return inverse, logs


def updates_kernel(
    rows, inverse_ref, left_ref, right_ref, left_rows_ref, vector_ref,
    logs_ref, tail_ref, up_ref, down_ref, link_ref,
):
    size = up_ref.shape[1]
    mine = lax.axis_index("rows") * rows + lax.broadcasted_iota(jnp.int32, (rows, size), 0)
    pick = (lax.broadcasted_iota(jnp.int32, (rows, size), 1) == mine).astype(jnp.float32)
    both = jnp.concatenate([left_rows_ref[...], dot(pick, right_ref[...], (1, 1))])
    solved = dot(both, inverse_ref[...], (1, 0))
    from_right = dot(solved, right_ref[...], (1, 0))
    up_ref[0:rows, :] = dot(solved[0:rows], left_ref[...], (1, 1))
    link_ref[...] = -from_right[0:rows]
    down_ref[0:rows, :] = from_right[rows:]
    vector = dot(vector_ref[...], solved, (1, 1))
    up_ref[rows:, :] = jnp.zeros((8, size), jnp.float32)
    up_ref[rows:, 0:rows] = vector[:, 0:rows]
    up_ref[rows:, size - TILE:] = logs_ref[...] - tail_ref[:, size - TILE:]
    down_ref[rows:, :] = jnp.zeros((8, size), jnp.float32)
    down_ref[rows:, 0:rows] = vector[:, rows:]


def updates(inverse, left, right, left_rows, vector, logs, tail):
    rows, size = left_rows.shape
    message = jax.ShapeDtypeStruct((rows + 8, size), jnp.float32)
    return pl.pallas_call(
        functools.partial(updates_kernel, rows),
        out_shape=(message, message, jax.ShapeDtypeStruct((rows, size), jnp.float32)),
        in_specs=[pl.BlockSpec(memory_space=pltpu.VMEM)] * 7,
        out_specs=(pl.BlockSpec(memory_space=pltpu.VMEM),) * 3,
        compiler_params=pltpu.CompilerParams(vmem_limit_bytes=24 << 20),
    )(
        inverse, left, right, left_rows,
        jnp.broadcast_to(vector[None], (8, size)), logs, tail,
    )


def exchange_kernel(
    stride, local_up, count, parts, own_ref, up_ref, down_ref, link_ref,
    new_ref, diag_ref, tails_ref, left_ref, right_ref,
    got_up, got_down, got_left, got_right, slots,
    send_sem, recv_sem, gather_send, gather_recv, forward_send, forward_recv,
):
    group, me = lax.axis_index("tm"), lax.axis_index("rows")
    rows = link_ref.shape[0]
    below = lax.rem(group + count - stride, count)
    above = lax.rem(group + stride, count)
    partner = me + 1 - 2 * lax.rem(me, 2)

    barrier = pltpu.get_barrier_semaphore()
    for other in (below, above):
        pl.semaphore_signal(
            barrier, inc=1, device_id={"tm": other}, device_id_type=pl.DeviceIdType.MESH
        )
    for distance in range(1, parts):
        pl.semaphore_signal(
            barrier, inc=1, device_id={"rows": lax.rem(me + distance, parts)},
            device_id_type=pl.DeviceIdType.MESH,
        )
    pl.semaphore_wait(barrier, parts + 1)

    if local_up:
        sends_down, gets_down = group < count - 1, group > 0
    else:
        place = lax.rem(group, 2 * stride)
        gets_up, sends_up = place == 0, place == stride
        sends_down = jnp.logical_and(place == stride, group + stride < count)
        gets_down = jnp.logical_and(place == 0, group > 0)

    def over_time(source, target, number, other):
        return pltpu.make_async_remote_copy(
            src_ref=source, dst_ref=target, send_sem=send_sem.at[number],
            recv_sem=recv_sem.at[number], device_id={"tm": other},
            device_id_type=pl.DeviceIdType.MESH,
        )

    up = over_time(up_ref, got_up, 0, below)
    down = over_time(down_ref, got_down, 1, above)
    link_up = over_time(link_ref, got_right, 2, below)
    link_down = over_time(link_ref, got_left, 3, above)

    if not local_up:
        @pl.when(sends_up)
        def _():
            up.start()

    @pl.when(sends_down)
    def _():
        down.start()

    if not local_up:
        @pl.when(sends_up)
        def _():
            link_up.start()

    @pl.when(sends_down)
    def _():
        link_down.start()

    if local_up:
        new_ref[...] = own_ref[...] - up_ref[...]
    else:
        new_ref[...] = own_ref[...]

        @pl.when(gets_up)
        def _():
            up.wait_recv()
            new_ref[...] -= got_up[...]

    @pl.when(gets_down)
    def _():
        down.wait_recv()
        new_ref[...] -= got_down[...]

    def over_rows(source, slot, target, send, recv):
        return pltpu.make_async_remote_copy(
            src_ref=source, dst_ref=slots.at[slot], send_sem=send, recv_sem=recv,
            device_id={"rows": target}, device_id_type=pl.DeviceIdType.MESH,
        )

    chips = parts // 2
    sent = []
    for d in range(1, chips):
        target = lax.rem(me + 2 * d, parts)
        copy = over_rows(new_ref, me, target, gather_send.at[d], gather_recv.at[d])
        copy.start()
        sent.append(copy)
    forwards = [over_rows(new_ref, me, partner, forward_send.at[0], forward_recv.at[0])]
    forwards[0].start()
    slots[me] = new_ref[...]
    for d in range(1, chips):
        sent[d - 1].wait_recv()
        source = lax.rem(me + parts - 2 * d, parts)
        copy = over_rows(
            slots.at[source], source, partner, forward_send.at[d], forward_recv.at[d]
        )
        copy.start()
        forwards.append(copy)
    for copy in forwards:
        copy.wait_recv()
    for copy in sent + forwards:
        copy.wait_send()
    for part in range(parts):
        diag_ref[part * rows:(part + 1) * rows, :] = slots[part, 0:rows, :]
        tails_ref[part * 8:(part + 1) * 8, :] = slots[part, rows:, :]

    left_ref[...] = jnp.zeros(left_ref.shape, jnp.float32)

    @pl.when(gets_down)
    def _():
        link_down.wait_recv()
        left_ref[...] = got_left[...]

    if local_up:
        right_ref[...] = link_ref[...]
    else:
        right_ref[...] = jnp.zeros(right_ref.shape, jnp.float32)

        @pl.when(gets_up)
        def _():
            link_up.wait_recv()
            right_ref[...] = got_right[...]

        @pl.when(sends_up)
        def _():
            up.wait_send()
            link_up.wait_send()

    @pl.when(sends_down)
    def _():
        down.wait_send()
        link_down.wait_send()


def exchanged(number, stride, local_up, own, up, down, link):
    rows, size = link.shape
    count, parts = lax.axis_size("tm"), lax.axis_size("rows")
    message = jax.ShapeDtypeStruct((rows + 8, size), jnp.float32)
    part = jax.ShapeDtypeStruct((rows, size), jnp.float32)
    new, diag, tails, left, right = pl.pallas_call(
        functools.partial(exchange_kernel, stride, local_up, count, parts),
        out_shape=(
            message, jax.ShapeDtypeStruct((size, size), jnp.float32),
            jax.ShapeDtypeStruct((8 * parts, size), jnp.float32), part, part,
        ),
        in_specs=[pl.BlockSpec(memory_space=pltpu.VMEM)] * 4,
        out_specs=(pl.BlockSpec(memory_space=pltpu.VMEM),) * 5,
        scratch_shapes=[
            pltpu.VMEM((rows + 8, size), jnp.float32),
            pltpu.VMEM((rows + 8, size), jnp.float32),
            pltpu.VMEM((rows, size), jnp.float32),
            pltpu.VMEM((rows, size), jnp.float32),
            pltpu.VMEM((parts, rows + 8, size), jnp.float32),
            pltpu.SemaphoreType.DMA((4,)),
            pltpu.SemaphoreType.DMA((4,)),
            pltpu.SemaphoreType.DMA((parts // 2,)),
            pltpu.SemaphoreType.DMA((parts // 2,)),
            pltpu.SemaphoreType.DMA((parts // 2,)),
            pltpu.SemaphoreType.DMA((parts // 2,)),
        ],
        compiler_params=pltpu.CompilerParams(
            collective_id=number, has_side_effects=True, vmem_limit_bytes=24 << 20
        ),
    )(own, up, down, link)
    vector = tails.reshape(parts, 8, size)[:, 0, :rows].reshape(size)
    return new, diag, vector, left, right


def product(left_part, right_part):
    return jnp.dot(left_part, right_part, precision=HIGHEST)


def shifted(block, axis, distance):
    devices = range(lax.axis_size(axis))
    route = [(i - distance, i) for i in devices if i - distance in devices]
    return lax.ppermute(block, axis, route)


def local(diag_blocks, coupling, rhs):
    group_steps, rows, size = diag_blocks.shape
    group_count = lax.axis_size("tm")
    group_index = lax.axis_index("tm")
    row_start = lax.axis_index("rows") * rows
    level_count = group_count.bit_length() - 1
    not_last = jnp.where(group_index == group_count - 1, 0.0, 1.0).astype(jnp.float32)

    def my_rows(matrix):
        return lax.dynamic_slice_in_dim(matrix, row_start, rows, 0)

    def gathered(part):
        return lax.all_gather(part, "rows", axis=0, tiled=True)

    def as_row(vector):
        return jnp.pad(vector[None], ((0, 7), (0, size - rows)))

    def eliminated(diag, vector, left_part, right_part, tail):
        left, right = gathered(left_part), gathered(right_part)
        inverse, logs = inverted(diag)
        up, down, link = updates(inverse, left, right, left_part, vector, logs, tail)
        return up, down, link, (inverse, left, right, vector)

    pivot, left, right, vector = lax.optimization_barrier((
        gathered(diag_blocks[1]), coupling[0], coupling[1] * not_last, as_row(rhs[1])
    ))
    vector = gathered(vector).reshape(-1, 8, size)[:, 0, :rows].reshape(size)
    up, down, link, chain = eliminated(
        pivot, vector, left, right, jnp.zeros((8, size), jnp.float32)
    )
    own = jnp.concatenate([diag_blocks[0], as_row(rhs[0])])
    own, diag, vector, left, right = exchanged(0, 1, True, own, up, down, link)
    levels_kept = []
    for level_index in range(level_count):
        stride = 1 << level_index
        is_pivot = group_index % (2 * stride) == stride
        up, down, link, kept = eliminated(diag, vector, left, right, own[rows:])
        levels_kept.append((is_pivot, kept))
        own, diag, vector, left, right = exchanged(
            level_index + 1, stride, False, own, up, down, link
        )
    tail = own[rows:]
    inverse, logs = inverted(diag)
    total = jnp.sum(logs[0] - tail[0, size - TILE:])
    states = jnp.concatenate([product(inverse, vector), jnp.full((TILE,), total)])
    for level_index in reversed(range(level_count)):
        stride = 1 << level_index
        is_pivot, (inverse, left, right, vector) = levels_kept[level_index]
        below = shifted(states, "tm", stride)
        above = shifted(states, "tm", -stride)
        new_state = product(
            inverse, vector - product(below[:size], left) - product(right, above[:size])
        )
        states = jnp.where(is_pivot, jnp.concatenate([new_state, below[size:]]), states)
    total = states[size]
    states = states[:size]
    inverse, left, right, vector = chain
    following = shifted(states, "tm", -1)
    following = product(inverse, vector - product(states, left) - product(right, following))
    solution = jnp.stack([my_rows(states), my_rows(following)], axis=0)
    return (solution, total / (group_steps * group_count * size))


def solution(mesh):
    in_specs = (P("tm", "rows", None), P("tm", "rows", None), P("tm", "rows"))
    out_specs = (P("tm", "rows"), P())
    return jax.shard_map(local, mesh=mesh, in_specs=in_specs, out_specs=out_specs, check_vma=False)
```
